256 devices in a mesh: dp: 16 (over y, x_hi, core), mp: 16 (over x_lo, z).
Axes of the slice: x: 4 (x_hi: 2, x_lo: 2; x = x_hi * 2 + x_lo), y: 4, z: 8, core: 2. Of those that a mesh axis runs over, the one named last changes fastest.
Arguments:
- activations: bfloat16 [16384, 4096], P('dp', 'mp'), may hold values from -6 to 6
- out_grads: bfloat16 [16384, 512], P(('dp', 'mp')), may hold values from -6 to 6
- doc_slot: int32 [16384], P('dp'), may hold values from 0 to 7
- input_eigenvectors: bfloat16 [4096, 4096], P(None, 'mp'), as said below
- eigen_out: bfloat16 [512, 512], replicated, as said below
- query_tiles: bfloat16 [32, 512, 4096], P(None, 'dp', 'mp'), may hold values from -6 to 6
- query_pick: int32 [16], replicated, may hold values from 0 to 31, as said below
Outputs:
- preconditioned: bfloat16 [4096, 16, 512], P('mp', None, 'dp')
The draws below stay inside these ranges and needn't reach their ends.
Inputs may be any that keep to these rules, and one draw needn't show every extreme that they name: `doc_slot`: numbers name documents within the row's own group. `query_pick`: 16 different indices, among them 0 and 31, in no particular order. `input_eigenvectors`: Real-valued basis matrix with columns of unequal length. `eigen_out`: Real-valued basis matrix with columns of unequal length.
All inputs are finite; a program needn't handle non-finite values.
Results may differ from the reference program's by a relative error of at most 0.011.
Values may be sent and summed in bfloat16 or wider, within the bound.
A program may use at most 64 MiB of HBM per device.

```python
import math
import jax
import jax.numpy as jnp
from jax import lax

D = 4096
E = 512
ROWS_G = 1024
DOC_G = 8
NQ = 32
NSEL = 16
ROWS = 16384
N_DP = 16


def draw_input_eigenvectors(key, part):
    key_main, key_cols = jax.random.split(jax.random.fold_in(key, 17), 2)
    col_scale = jnp.exp(jax.random.uniform(key_cols, (1, D), jnp.float32, math.log(0.3), math.log(3.0)))
    entries = jax.random.normal(key_main, (D, D), jnp.float32)
    return (entries * col_scale / math.sqrt(D)).astype(jnp.bfloat16)


def draw_eigen_out(key, part):
    key_main, key_cols = jax.random.split(jax.random.fold_in(key, 29), 2)
    col_scale = jnp.exp(jax.random.uniform(key_cols, (1, E), jnp.float32, math.log(0.3), math.log(3.0)))
    entries = jax.random.normal(key_main, (E, E), jnp.float32)
    return (entries * col_scale * 0.1 / math.sqrt(E)).astype(jnp.bfloat16)


def draw_query_pick(key, part):
    key_middle, key_order = jax.random.split(jax.random.fold_in(key, 41), 2)
    middle = jax.random.permutation(key_middle, NQ - 2).astype(jnp.int32) + 1
    ends = jnp.array([0, NQ - 1], jnp.int32)
    picked = jnp.concatenate([ends, middle[:NSEL - 2]])
    order = jax.random.permutation(key_order, NSEL)
    return jnp.take(picked, order, axis=0).astype(jnp.int32)


def place_ends(values, own_key, smallest, top_value):
    spot = [jax.random.randint(jax.random.fold_in(own_key, axis), (), 0, length) for axis, length in enumerate(values.shape)]
    longest = values.shape.index(max(values.shape))
    next_to = spot[:longest] + [(spot[longest] + 1) % values.shape[longest]] + spot[longest + 1:]
    return values.at[tuple(spot)].set(smallest).at[tuple(next_to)].set(top_value)


def shard_levels(key, dims, pieces, least, high):
    def one(position, shards_of):
        steps = jax.random.uniform(jax.random.fold_in(jax.random.fold_in(key, 6), position), (shards_of,), jnp.float32, least / len(pieces), high / len(pieces))
        return jnp.repeat(jnp.exp(steps), dims[position] // shards_of).reshape((-1,) + (1,) * (len(dims) - position - 1))

    gain = one(*pieces[0])
    for cut in pieces[1:]:
        gain = gain * one(*cut)
    return gain


def normal_values(own_key, extent, width, most, pieces=(), held_as=jnp.bfloat16):
    drawn = width * jax.random.normal(own_key, extent, jnp.float32)
    if pieces:
        drawn = drawn * shard_levels(own_key, extent, pieces, -0.22, 0.18)
    return jnp.clip(drawn, -most, most).astype(held_as)


def setup_inputs(seed: int = 0) -> dict:
    splits = jax.random.split(jax.random.key(seed), 8)
    activations = normal_values(splits[0], (ROWS, D), 1.0, 6.0, ((0, 16), (1, 16)))
    out_grads = normal_values(splits[1], (ROWS, E), 1.0, 6.0, ((0, 256),))
    doc_slot = place_ends(jax.random.randint(splits[2], (ROWS,), 0, DOC_G), jax.random.fold_in(splits[2], 1), 0, DOC_G - 1).astype(jnp.int32)
    input_eigenvectors = draw_input_eigenvectors(jax.random.fold_in(splits[7], 71), 0)
    eigen_out = draw_eigen_out(jax.random.fold_in(splits[7], 71), 0)
    query_tiles = normal_values(splits[5], (NQ, E, D), 1.0, 6.0, ((1, 16), (2, 16)))
    query_pick = draw_query_pick(jax.random.fold_in(splits[7], 71), 0)
    return dict(activations=activations, out_grads=out_grads, doc_slot=doc_slot, input_eigenvectors=input_eigenvectors, eigen_out=eigen_out, query_tiles=query_tiles, query_pick=query_pick)


DAMPING = 0.1


def reference(activations, out_grads, doc_slot, input_eigenvectors, eigen_out, query_tiles, query_pick):
    rotated_in = jnp.dot(activations, input_eigenvectors, preferred_element_type=jnp.float32).astype(jnp.bfloat16)
    rotated_out = jnp.dot(out_grads, eigen_out, preferred_element_type=jnp.float32).astype(jnp.bfloat16)
    group_in = rotated_in.reshape(N_DP, ROWS_G, D)
    group_out = rotated_out.reshape(N_DP, ROWS_G, E)
    group_slot = doc_slot.reshape(N_DP, ROWS_G)

    def single_group(packed):
        slot_rows, out_rows, in_rows = packed
        onehot = (slot_rows[None, :] == jnp.arange(DOC_G, dtype=jnp.int32)[:, None]).astype(jnp.float32)
        masked_entries = onehot[:, :, None] * out_rows.astype(jnp.float32)[None]
        doc_grad = jnp.einsum('nre,rk->nek', masked_entries, in_rows.astype(jnp.float32))
        return jnp.sum(doc_grad * doc_grad, axis=0)

    squared_entries = lax.map(single_group, (group_slot, group_out, group_in))
    eigen_vals = jnp.sum(squared_entries, axis=0) / (DOC_G * N_DP)
    chosen = jnp.take(query_tiles, query_pick, axis=0).astype(jnp.float32)
    rescaled_gradient = (chosen / (eigen_vals[None] + DAMPING)).astype(jnp.bfloat16)
    final_output = jnp.einsum('qu,atu->qat', input_eigenvectors.astype(jnp.float32), rescaled_gradient.astype(jnp.float32))
    return final_output.astype(jnp.bfloat16)
```

```python
import functools

import jax
import jax.numpy as jnp
from jax import lax
from jax.experimental import pallas as pl
from jax.experimental.pallas import tpu as pltpu
from jax.sharding import PartitionSpec as P

DOC_G = 8
DAMPING = 0.1
PAIR = 2
UNITS = 4
MESH = pl.DeviceIdType.MESH
F32 = jnp.float32
BF16 = jnp.bfloat16


def fused(
    n_dp,
    n_mp,
    act,
    og,
    slots,
    vecs,
    eo,
    tiles,
    pick,
    out,
    a_buf,
    v_buf,
    og_buf,
    eo_buf,
    q_buf,
    ro_buf,
    own_buf,
    psend,
    precv,
    acc,
    sq_send,
    sq_own,
    sq_recv,
    sc,
    r_send,
    r_recv,
    load_sem,
    a_send_sem,
    a_recv_sem,
    v_send_sem,
    v_recv_sem,
    o_send_sem,
    o_recv_sem,
    ox_send_sem,
    ox_recv_sem,
    p_send_sem,
    p_recv_sem,
    sq_send_sem,
    sq_recv_sem,
    sc_sems,
    r_send_sem,
    r_recv_sem,
):
    nz = n_mp // PAIR
    far = nz // 2
    cols = act.shape[1]
    unit = a_buf.shape[1]
    part = og.shape[0]
    owner = tiles.shape[1]
    nsel = pick.shape[0]
    half = nsel * owner // 2
    dp = lax.axis_index("dp")
    mp = lax.axis_index("mp")
    b = mp // nz
    z = lax.rem(mp, nz)
    right = b * nz + lax.rem(z + 1, nz)
    left = b * nz + lax.rem(z + nz - 1, nz)
    pair = (1 - b) * nz + z
    ways = (right, left)

    def hops(way, u):
        return far if (way + u) % 2 == 0 else far - 1

    def from_z(way, s):
        return s + 1 if way == 0 else nz - 1 - s

    def remote(src, dst, ssem, rsem, where):
        return pltpu.make_async_remote_copy(
            src_ref=src,
            dst_ref=dst,
            send_sem=ssem,
            recv_sem=rsem,
            device_id=where,
            device_id_type=MESH,
        )

    loads = []

    def load(src, dst):
        copy = pltpu.make_async_copy(src, dst, load_sem.at[len(loads)])
        copy.start()
        loads.append(copy)
        return copy

    load_og = load(og, og_buf)
    load_eo = load(eo, eo_buf)
    load_a = [load(act.at[pl.ds(u * unit, unit)], a_buf.at[u, :, pl.ds(0, cols)]) for u in range(UNITS)]

    def k_rows(bb, r):
        return pl.ds(pl.multiple_of((bb * nz + lax.rem(z - r + nz, nz)) * cols, cols), cols)

    load_v = [
        load(vecs.at[k_rows(b, r)], v_buf.at[pl.ds(r * cols, cols), pl.ds(0, cols)]) for r in range(nz)
    ]
    load_q = load(tiles, q_buf)

    barrier = pltpu.get_barrier_semaphore()
    for peer in (right, left, pair):
        pl.semaphore_signal(barrier, inc=1, device_id={"mp": peer}, device_id_type=MESH)
    for o in range(1, n_dp):
        pl.semaphore_signal(
            barrier, inc=1, device_id={"dp": lax.rem(dp + o, n_dp)}, device_id_type=MESH
        )
    pl.semaphore_wait(barrier, 3 + n_dp - 1)

    def a_copy(way, s, u):
        dst = a_buf.at[u, :, pl.ds(from_z(way, s) * cols, cols)]
        if s == 0:
            src = act.at[pl.ds(u * unit, unit)]
        else:
            src = a_buf.at[u, :, pl.ds(from_z(way, s - 1) * cols, cols)]
        return remote(
            src, dst, a_send_sem.at[way, s, u], a_recv_sem.at[way, s, u], {"mp": ways[way]}
        )

    for u in range(UNITS):
        for way in range(2):
            a_copy(way, 0, u).start()

    def v_copy(r):
        return remote(
            vecs.at[k_rows(1 - b, r)],
            v_buf.at[pl.ds(r * cols, cols), pl.ds(cols, cols)],
            v_send_sem.at[r],
            v_recv_sem.at[r],
            {"mp": pair},
        )

    for r in range(nz):
        v_copy(r).start()

    def o_rows(bb, r):
        return pl.ds(pl.multiple_of((bb * nz + lax.rem(z - r + nz, nz)) * part, part), part)

    def o_copy(way, s):
        prev = 0 if s == 0 else from_z(way, s - 1)
        src = ro_buf.at[o_rows(b, prev)]
        return remote(
            src, src, o_send_sem.at[way, s], o_recv_sem.at[way, s], {"mp": ways[way]}
        )

    def ox_copy(r):
        src = ro_buf.at[o_rows(b, r)]
        return remote(src, src, ox_send_sem.at[r], ox_recv_sem.at[r], {"mp": pair})

    def o_arrival(way, s):
        dst = ro_buf.at[o_rows(b, from_z(way, s))]
        return remote(
            dst, dst, o_send_sem.at[way, s], o_recv_sem.at[way, s], {"mp": ways[way]}
        )

    def ox_arrival(r):
        dst = ro_buf.at[o_rows(1 - b, r)]
        return remote(dst, dst, ox_send_sem.at[r], ox_recv_sem.at[r], {"mp": pair})

    load_og.wait()
    load_eo.wait()
    ro_buf[o_rows(b, 0), :] = jnp.dot(
        og_buf[...], eo_buf[...], preferred_element_type=F32
    ).astype(BF16)
    for way in range(2):
        o_copy(way, 0).start()
    ox_copy(0).start()

    for s in range(1, far):
        for u in range(UNITS):
            for way in range(2):
                a_copy(way, s - 1, u).wait_recv()
                if s < hops(way, u):
                    a_copy(way, s, u).start()
        for way in range(2):
            if s - 1 < hops(way, 0):
                o_arrival(way, s - 1).wait_recv()
                if s < hops(way, 0):
                    o_copy(way, s).start()
                ox_copy(from_z(way, s - 1)).start()
    o_arrival(0, far - 1).wait_recv()
    ox_copy(far).start()

    for copy in load_a + load_v + [load_q]:
        copy.wait()
    for r in range(nz):
        v_copy(r).wait_recv()
    for r in range(nz):
        ox_arrival(r).wait_recv()

    def p_copy(u):
        return remote(
            psend.at[u], precv.at[u], p_send_sem.at[u], p_recv_sem.at[u], {"mp": pair}
        )

    def rotate(u):
        a_copy(u % 2, far - 1, u).wait_recv()
        prod = jnp.dot(a_buf[u], v_buf[...], preferred_element_type=F32)
        own_buf[u] = prod[:, :cols]
        psend[u] = prod[:, cols:].astype(BF16)
        p_copy(u).start()

    def document_grads(u):
        p_copy(u).wait_recv()
        rot_t = (own_buf[u] + precv[u].astype(F32)).T.astype(BF16)
        where = slots[:, u * unit : (u + 1) * unit]
        rows = ro_buf[u * unit : (u + 1) * unit, :]

        def one(n, carry):
            mask = (where == n).astype(F32).astype(BF16)
            grad = jnp.dot(rot_t * mask, rows, preferred_element_type=F32)
            if u == 0:
                acc[n] = grad
            elif u < UNITS - 1:
                acc[n] += grad
            else:
                grad += acc[n]
                carry = carry + grad * grad
            return carry

        if u < UNITS - 1:
            lax.fori_loop(0, DOC_G, lambda n, c: (one(n, c), c)[1], 0)
            return None
        total = jnp.zeros(acc.shape[1:], F32)
        for n in range(DOC_G):
            total = one(n, total)
        return total

    for u in range(UNITS):
        rotate(u)
        if u > 0:
            document_grads(u - 1)
    squares = document_grads(UNITS - 1).T
    sq_own[...] = squares.reshape(sq_own.shape)
    sq_send[...] = squares.reshape(sq_send.shape).astype(BF16)

    def sq_copy(o):
        to = lax.rem(dp + o, n_dp)
        return remote(
            sq_send.at[to], sq_recv.at[o - 1], sq_send_sem.at[o - 1], sq_recv_sem.at[o - 1], {"dp": to}
        )

    for o in range(1, n_dp):
        sq_copy(o).start()
    summed = sq_own[dp]
    for o in range(1, n_dp):
        sq_copy(o).wait_recv()
        summed = summed + sq_recv[o - 1].astype(F32)
    damped = summed / (DOC_G * n_dp) + DAMPING
    for s in range(nsel):
        sc[s * owner : (s + 1) * owner, :cols] = (q_buf[pick[s]].astype(F32) / damped).astype(BF16)

    sc_copy = remote(
        sc.at[:, pl.ds(0, cols)], sc.at[:, pl.ds(cols, cols)], sc_sems.at[0], sc_sems.at[1], {"mp": pair}
    )
    sc_copy.start()
    sc_copy.wait_recv()

    def product(r, h):
        return lax.dot_general(
            v_buf[r * cols : (r + 1) * cols, :],
            sc[h * half : (h + 1) * half, :],
            (((1,), (1,)), ((), ())),
            preferred_element_type=F32,
        )

    def r_copy(way, t, h):
        return remote(
            r_send.at[way, h, t],
            r_recv.at[way, h, t],
            r_send_sem.at[way, h, t],
            r_recv_sem.at[way, h, t],
            {"mp": ways[way]},
        )

    for t in range(far):
        for h in range(2):
            for way in range(2):
                reach = hops(way, h)
                if t >= reach:
                    continue
                r = nz - reach + t if way == 0 else reach - t
                mine = product(r, h)
                if t > 0:
                    r_copy(way, t - 1, h).wait_recv()
                    mine = mine + r_recv[way, h, t - 1].astype(F32)
                r_send[way, h, t] = mine.astype(BF16)
                r_copy(way, t, h).start()
    for h in range(2):
        mine = product(0, h)
        for way in range(2):
            last = hops(way, h) - 1
            r_copy(way, last, h).wait_recv()
            mine = mine + r_recv[way, h, last].astype(F32)
        out[:, h * half : (h + 1) * half] = mine.astype(BF16)

    for u in range(UNITS):
        for way in range(2):
            for s in range(hops(way, u)):
                a_copy(way, s, u).wait_send()
        p_copy(u).wait_send()
    for r in range(nz):
        v_copy(r).wait_send()
        ox_copy(r).wait_send()
    for way in range(2):
        for s in range(hops(way, 0)):
            o_copy(way, s).wait_send()
        for h in range(2):
            for t in range(hops(way, h)):
                r_copy(way, t, h).wait_send()
    for o in range(1, n_dp):
        sq_copy(o).wait_send()
    sc_copy.wait_send()


def shards(n_dp, n_mp, act, og, doc_slot, vecs, eo, tiles, pick):
    rows, cols = act.shape
    nz = n_mp // PAIR
    far = nz // 2
    e = eo.shape[0]
    unit = rows // UNITS
    owner = tiles.shape[1]
    nsel = pick.shape[0]
    wide = nsel * owner
    vmem = pl.BlockSpec(memory_space=pltpu.VMEM)
    anywhere = pl.BlockSpec(memory_space=pl.ANY)
    dma = pltpu.SemaphoreType.DMA
    flat = pl.pallas_call(
        functools.partial(fused, n_dp, n_mp),
        out_shape=jax.ShapeDtypeStruct((cols, wide), BF16),
        in_specs=[
            anywhere,
            anywhere,
            vmem,
            anywhere,
            anywhere,
            anywhere,
            pl.BlockSpec(memory_space=pltpu.SMEM),
        ],
        out_specs=vmem,
        scratch_shapes=[
            pltpu.VMEM((UNITS, unit, nz * cols), BF16),
            pltpu.VMEM((nz * cols, 2 * cols), BF16),
            pltpu.VMEM(og.shape, BF16),
            pltpu.VMEM(eo.shape, BF16),
            pltpu.VMEM(tiles.shape, BF16),
            pltpu.VMEM((rows, e), BF16),
            pltpu.VMEM((UNITS, unit, cols), F32),
            pltpu.VMEM((UNITS, unit, cols), BF16),
            pltpu.VMEM((UNITS, unit, cols), BF16),
            pltpu.VMEM((DOC_G, cols, e), F32),
            pltpu.VMEM((n_dp, owner, cols), BF16),
            pltpu.VMEM((n_dp, owner, cols), F32),
            pltpu.VMEM((n_dp - 1, owner, cols), BF16),
            pltpu.VMEM((wide, 2 * cols), BF16),
            pltpu.VMEM((2, 2, far, cols, wide // 2), BF16),
            pltpu.VMEM((2, 2, far, cols, wide // 2), BF16),
            dma((3 + UNITS + nz,)),
            dma((2, far, UNITS)),
            dma((2, far, UNITS)),
            dma((nz,)),
            dma((nz,)),
            dma((2, far)),
            dma((2, far)),
            dma((nz,)),
            dma((nz,)),
            dma((UNITS,)),
            dma((UNITS,)),
            dma((n_dp - 1,)),
            dma((n_dp - 1,)),
            dma((2,)),
            dma((2, 2, far)),
            dma((2, 2, far)),
        ],
        compiler_params=pltpu.CompilerParams(
            collective_id=0, has_side_effects=True, vmem_limit_bytes=48 * 1024 * 1024
        ),
        cost_estimate=pl.CostEstimate(
            flops=6_000_000_000, bytes_accessed=8_000_000, transcendentals=0
        ),
    )(act, og, doc_slot.reshape(1, rows), vecs, eo, tiles, pick)
    return flat.reshape(cols, nsel, owner)


def solution(mesh):
    in_specs = (
        P("dp", "mp"),
        P(("dp", "mp"), None),
        P("dp"),
        P(None, "mp"),
        P(),
        P(None, "dp", "mp"),
        P(),
    )
    out_specs = P("mp", None, "dp")
    body = functools.partial(shards, mesh.shape["dp"], mesh.shape["mp"])
    return jax.shard_map(body, mesh=mesh, in_specs=in_specs, out_specs=out_specs, check_vma=False)
```
